256 devices in a mesh: ed: 16 (over z, core), ep: 16 (over y, x).
Axes of the slice: x: 4, y: 4, z: 8, core: 2. Of those that a mesh axis runs over, the one named last changes fastest.
Arguments:
- out_grad: bfloat16 [32768, 3584], P(('ed', 'ep')), may hold values from -4.1 to 4.1
- routes: int32 [32768, 2], P(('ed', 'ep')), may hold values from 0 to 15, all different within a row; in each aligned block of 128 rows (0 to 127, 128 to 255, ...) at most 32 rows name the same one
- gates: bfloat16 [32768, 2], P(('ed', 'ep')), may hold values from 0.049804688 to 0.59765625
- pre_acts: bfloat16 [16, 16, 16, 32, 2048], P('ed', 'ep'), may hold values from -6 to 6
- down_weight: bfloat16 [16, 1024, 3584], P('ep'), may hold values from -0.1875 to 0.1875
- history: float32 [16, 16, 16], P('ed', 'ep'), may hold values from 4 to 32
Outputs:
- pre_grad: bfloat16 [16, 16, 16, 32, 2048], P('ed', 'ep')
- wgrad: float32 [16, 3584, 1024], P('ep', 'ed')
- new_history: float32 [16, 16], P('ep')
- gate_grad: float32 [32768, 2], P(('ed', 'ep'))
The draws below stay inside these ranges and needn't reach their ends.
Inputs may be any that keep to these rules, and one draw needn't show every extreme that they name: `routes`: each token names 2 different experts; among the 128 rows of one device no expert is named more than 32 times, and in some device's rows one expert is named exactly 32 times.
All inputs are finite; a program needn't handle non-finite values.
Results may differ from the reference program's by a relative error of at most 0.025.
Values may be sent and summed in bfloat16 or wider, within the bound.
No kernel may reach another device: no remote copies, remote signals or barrier semaphores. Data moves between devices by JAX's collectives and lax.ppermute only.
A program may use at most 128 MiB of HBM per device.

```python
import math
import jax
import jax.numpy as jnp
import numpy as np
from jax import lax

D = 3584
EXPERT_FF = 1024
TOPW = 2
HIST = 16
TOK_DEV = 128
EXPERTS = 16
CAP = 32
TOKENS = 32768
N_ED = 16
N_EP = 16


def draw_out_grad(key, part):
    key = jax.random.fold_in(key, 7)
    first, second = jax.random.split(key, 2)
    column = jnp.arange(D, dtype=jnp.float32) / max(D - 1, 1)
    rough = jnp.exp(jax.random.uniform(second, (D,), jnp.float32, -0.4, 0.4))
    column_scale = 0.1 * jnp.exp(1.5 * column) * rough
    base = jnp.clip(jax.random.normal(first, (TOKENS, D), jnp.float32), -6.0, 6.0)
    values = base * column_scale[None, :]
    return values.astype(jnp.bfloat16)


def block_levels(stream_key, shape, shards, low, top_value):
    def one(axis_at, blocks):
        heights = jax.random.uniform(jax.random.fold_in(jax.random.fold_in(stream_key, 6), axis_at), (blocks,), jnp.float32, low / len(shards), top_value / len(shards))
        return jnp.repeat(jnp.exp(heights), shape[axis_at] // blocks).reshape((-1,) + (1,) * (len(shape) - axis_at - 1))

    gain = one(*shards[0])
    for cut in shards[1:]:
        gain = gain * one(*cut)
    return gain


def assign_block(key, own, number, rows, count, top, bound, skew):
    ranking = jax.random.permutation(key, count)
    heavy_load, usual = portions_of(count, rows * top, bound, skew, True), portions_of(count, rows * top, bound, skew, False)
    places = jnp.arange(count)

    def named(lengths, offset_by):
        used = int((lengths > 0).sum())
        fixed = max(1, used // 4)
        moved = fixed + (places - fixed + offset_by * (used - fixed)) % max(1, count - fixed)
        return jnp.zeros((count,), jnp.int32).at[ranking[jnp.where(places < fixed, places, moved)]].set(jnp.asarray(lengths, jnp.int32))

    lengths = jnp.where(number % 4 == 0, named(heavy_load, number // 4), named(usual, number - number // 4 - 1))
    mixed = jax.random.permutation(jax.random.fold_in(own, 3), count)
    giver, sink = mixed[0:count // 2 * 2:2], mixed[1:count // 2 * 2:2]
    room = jnp.minimum(lengths[giver] - 1, bound - lengths[sink]) // 2
    room = jnp.where((giver == ranking[0]) | (sink == ranking[0]) | (lengths[sink] == 0), 0, jnp.maximum(room, 0))
    moved = jax.random.randint(jax.random.fold_in(own, 4), (count // 2,), 0, 1 << 20) % (room + 1)
    lengths = lengths.at[giver].add(-moved).at[sink].add(moved)
    labels = jnp.searchsorted(jnp.cumsum(lengths), jnp.arange(rows * top), side="right").astype(jnp.int32)
    listing = labels.reshape(top, rows).T
    listing = listing[jax.random.permutation(jax.random.fold_in(own, 1), rows)]
    offset_by = jax.random.randint(jax.random.fold_in(own, 2), (rows, 1), 0, top)
    return jnp.take_along_axis(listing, (jnp.arange(top)[None, :] + offset_by) % top, axis=1)


def portions_of(number_of, total, most, skew, full):
    portions = [(1 << 20) // math.isqrt(standing ** skew) + 1 for standing in range(1, number_of + 1)]
    largest = most if full else min(most, max(-(-total // number_of), total * portions[0] // sum(portions)))
    least = 1 if total - largest >= number_of - 1 else 0
    given, surplus = [largest] + [least] * (number_of - 1), total - largest - least * (number_of - 1)
    while surplus > 0:
        free = [i for i in range(1, number_of) if given[i] < largest] or [i for i in range(1, number_of) if given[i] < most]
        pool, budget = sum([portions[i] for i in free]), surplus
        for i in free:
            addition = min(most - given[i], max(1, budget * portions[i] // pool), surplus)
            given[i] = given[i] + addition
            surplus = surplus - addition
    return np.array(given)


def noise(stream_key, shape, scale, limit, shards=(), held_as=jnp.bfloat16):
    level = block_levels(stream_key, shape, shards, -0.22, 0.18) if shards else 1.0
    entries = jax.random.normal(stream_key, shape, jnp.float32) * scale * level
    return jnp.minimum(jnp.maximum(entries, -limit), limit).astype(held_as)


def setup_inputs(seed: int = 0) -> dict:
    arg_keys = jax.random.split(jax.random.key(seed), 7)
    out_grad = draw_out_grad(jax.random.fold_in(arg_keys[6], 71), 0)
    routes_keys = jax.random.split(jax.random.fold_in(arg_keys[1], 1), TOKENS // TOK_DEV)
    routes_turns = jax.random.permutation(jax.random.fold_in(arg_keys[1], 3), TOKENS // TOK_DEV)
    routes = jax.vmap(lambda own, number: assign_block(jax.random.fold_in(arg_keys[1], 2), own, number, TOK_DEV, EXPERTS, TOPW, CAP, 2))(routes_keys, routes_turns).reshape((TOKENS, TOPW))
    gates = jnp.clip(0.049804688 + 0.54785156 * jax.random.uniform(arg_keys[2], (TOKENS, TOPW), jnp.float32) ** block_levels(arg_keys[2], (TOKENS, TOPW), ((0, 256),), -0.2, 0.2), 0.049804688, 0.59765625).astype(jnp.bfloat16)
    pre_acts = noise(arg_keys[3], (N_ED, EXPERTS, N_EP, CAP, 2 * EXPERT_FF), 1.0, 6.0, ((0, 16), (1, 16)))
    down_weight = noise(arg_keys[4], (EXPERTS, EXPERT_FF, D), EXPERT_FF ** -0.5, 0.1875, ((0, 16),))
    history = jnp.clip(jnp.exp(math.log(32.0) - 2.0794415 * jax.random.uniform(arg_keys[5], (N_ED, EXPERTS, HIST), jnp.float32) ** block_levels(arg_keys[5], (N_ED, EXPERTS, HIST), ((0, 16), (1, 16)), -0.2, 0.2)), 4.0, 32.0)
    return dict(out_grad=out_grad, routes=routes, gates=gates, pre_acts=pre_acts, down_weight=down_weight, history=history)


def route_slots(routes):
    flat = routes.reshape(N_ED * N_EP, TOK_DEV * TOPW)
    hits = (flat[:, :, None] == jnp.arange(EXPERTS, dtype=jnp.int32)[None, None, :]).astype(jnp.int32)
    before = jnp.cumsum(hits, axis=1) - hits
    return jnp.sum(before * hits, axis=2).reshape(TOKENS, TOPW)


def reference(out_grad, routes, gates, pre_acts, down_weight, history):
    slot = route_slots(routes)
    block = (jnp.arange(TOKENS, dtype=jnp.int32) // TOK_DEV)[:, None]
    replica = block // N_EP
    source = block % N_EP
    target = ((((replica * EXPERTS + routes) * N_EP + source) * CAP) + slot).reshape(-1).astype(jnp.int32)
    total = N_ED * EXPERTS * N_EP * CAP
    owner = jnp.arange(TOKENS * TOPW, dtype=jnp.int32) // TOPW
    table = jnp.zeros((total,), jnp.int32).at[target].set(owner + 1)
    picked = out_grad[jnp.maximum(table - 1, 0)]
    rows_all = jnp.where((table > 0)[:, None], picked, jnp.zeros_like(picked))
    rows_all = rows_all.reshape(N_ED, EXPERTS, N_EP * CAP, D)
    gate_all = jnp.zeros((total,), jnp.bfloat16).at[target].set(gates.reshape(-1))
    gate_all = gate_all.reshape(N_ED, EXPERTS, N_EP * CAP)
    pre_all = pre_acts.reshape(N_ED, EXPERTS, N_EP * CAP, 2 * EXPERT_FF)
    merged = jnp.max(history, axis=0)
    ref_amax = jnp.max(merged, axis=1)
    scale = 1.0 / ref_amax

    def per_expert(expert):
        weight = down_weight[expert]
        factor = scale[expert]

        def step(accum, rep):
            rows_in = rows_all[rep, expert]
            gate_row = gate_all[rep, expert].astype(jnp.float32)[:, None]
            pre_block = pre_all[rep, expert]
            gate_pre = pre_block[:, :EXPERT_FF].astype(jnp.float32)
            up_pre = pre_block[:, EXPERT_FF:].astype(jnp.float32)
            sigma = jax.nn.sigmoid(gate_pre)
            act = (gate_pre * sigma * up_pre).astype(jnp.bfloat16)
            weighted = (gate_row * act.astype(jnp.float32)).astype(jnp.bfloat16)
            raw = jnp.dot(rows_in, weight.T, preferred_element_type=jnp.float32)
            score = jnp.sum(act.astype(jnp.float32) * raw, axis=1)
            grad_act = gate_row * raw
            grad_gate = grad_act * up_pre * sigma * (1.0 + gate_pre * (1.0 - sigma))
            grad_up = grad_act * gate_pre * sigma
            grad_pre = jnp.concatenate([grad_gate, grad_up], axis=1).astype(jnp.bfloat16)
            term = jnp.dot(rows_in.T, weighted, preferred_element_type=jnp.float32)
            part = (factor * term).astype(jnp.bfloat16)
            part = lax.optimization_barrier(part)
            return accum + part.astype(jnp.float32), (grad_pre, score)

        accum, (grad_pre, score) = lax.scan(step, jnp.zeros((D, EXPERT_FF), jnp.float32), jnp.arange(N_ED, dtype=jnp.int32))
        return accum, grad_pre, score

    wgrad, grad_pre, score = lax.map(per_expert, jnp.arange(EXPERTS, dtype=jnp.int32))
    pre_grad = jnp.transpose(grad_pre, (1, 0, 2, 3)).reshape(N_ED, EXPERTS, N_EP, CAP, 2 * EXPERT_FF)
    new_amax = jnp.max(jnp.abs(wgrad), axis=(1, 2)) * ref_amax
    new_history = jnp.concatenate([merged[:, 1:], new_amax[:, None]], axis=1)
    score_flat = jnp.transpose(score, (1, 0, 2)).reshape(-1)
    gate_grad = score_flat[target].reshape(TOKENS, TOPW)
    return pre_grad, wgrad, new_history, gate_grad
```

```python
import functools

import jax
import jax.numpy as jnp
from jax import lax
from jax.experimental import pallas as pl
from jax.experimental.pallas import tpu as pltpu
from jax.sharding import PartitionSpec as P

LANES = 128
BF16 = jnp.bfloat16
F32 = jnp.float32
HOPS = (4, 3, -3, 2, -2, 1, -1, 0)


def block_order(size):
    me = lax.axis_index("ed")
    place, core = me // 2, me % 2
    spots = [2 * lax.rem(place + hop + size, size // 2) for hop in HOPS]
    return [spot + 1 - core for spot in spots] + [spot + core for spot in spots]


def dispatch_kernel(cap, routes_any, gates_any, grad_any, send_ref, hot0_ref, hot1_ref, routes_ref, gates_ref, grad_ref, held, sems):
    copies = [
        pltpu.make_async_copy(src, dst, sems.at[i])
        for i, (src, dst) in enumerate(
            [(routes_any, routes_ref), (gates_any, gates_ref), (grad_any, grad_ref)]
        )
    ]
    for copy in copies:
        copy.start()
    tokens, width = grad_ref.shape
    blocks = held.shape[0]
    block = width // blocks
    experts = send_ref.shape[0] // cap
    copies[0].wait()
    copies[1].wait()
    expert = lax.broadcasted_iota(jnp.int32, (experts, tokens), 0)
    one = routes_ref[0:1, :] == expert
    two = routes_ref[1:2, :] == expert
    named = jnp.where(one | two, 1.0, 0.0).astype(BF16)
    earlier = lax.broadcasted_iota(jnp.int32, (tokens, tokens), 0) < lax.broadcasted_iota(
        jnp.int32, (tokens, tokens), 1
    )
    before = jnp.dot(named, jnp.where(earlier, 1.0, 0.0).astype(BF16), preferred_element_type=F32)
    slots = lax.broadcasted_iota(jnp.int32, (experts, cap, tokens), 1)
    hit = slots == before.astype(jnp.int32)[:, None, :]
    gate0 = jnp.where(one, gates_ref[0:1, :].astype(F32), 0.0)
    gate1 = jnp.where(two, gates_ref[1:2, :].astype(F32), 0.0)
    rows = experts * cap
    hot0 = jnp.where(hit, jnp.where(one, 1.0, 0.0)[:, None, :], 0.0).reshape(rows, tokens)
    hot1 = jnp.where(hit, jnp.where(two, 1.0, 0.0)[:, None, :], 0.0).reshape(rows, tokens)
    gate = jnp.where(hit, (gate0 + gate1)[:, None, :], 0.0).reshape(rows, tokens)
    hot0_ref[...] = hot0.astype(BF16)
    hot1_ref[...] = hot1.astype(BF16)
    hot = (hot0 + hot1).astype(BF16)
    send_ref[:, width:] = jnp.dot(
        gate.astype(BF16), jnp.ones((tokens, LANES), BF16), preferred_element_type=F32
    ).astype(BF16)
    copies[2].wait()
    x = grad_ref[...].astype(F32)
    for b in range(blocks):
        held[b, :, :block] = x[:, b * block : (b + 1) * block]
    order = block_order(blocks)
    x = jnp.concatenate([held[i][:, :block] for i in order], axis=1).astype(BF16)
    send_ref[:, :width] = jnp.dot(hot, x, preferred_element_type=F32).astype(BF16)


def raw_kernel(rows_ref, pre_ref, weight_ref, grad_ref, score_ref, held):
    hidden, width = weight_ref.shape
    blocks = held.shape[0]
    block = width // blocks
    x = rows_ref[...].astype(F32)
    for i, b in enumerate(block_order(blocks)):
        held[b, :, :block] = x[:, i * block : (i + 1) * block]
    rows = jnp.concatenate([held[b][:, :block] for b in range(blocks)], axis=1).astype(BF16)
    gate = x[:, width : width + 1]
    score = None
    step = 256
    for n in range(0, hidden, step):
        raw = lax.dot_general(
            rows, weight_ref[n : n + step, :], (((1,), (1,)), ((), ())), preferred_element_type=F32
        )
        gate_pre = pre_ref[:, n : n + step].astype(F32)
        up_pre = pre_ref[:, hidden + n : hidden + n + step].astype(F32)
        sigma = jax.nn.sigmoid(gate_pre)
        swish = gate_pre * sigma
        act = (swish * up_pre).astype(BF16).astype(F32)
        part = jnp.sum(act * raw, axis=1, keepdims=True)
        score = part if score is None else score + part
        grad_act = gate * raw
        grad_gate = grad_act * up_pre * sigma * (1.0 + gate_pre * (1.0 - sigma))
        grad_ref[:, n : n + step] = grad_gate.astype(BF16)
        grad_ref[:, hidden + n : hidden + n + step] = (grad_act * swish).astype(BF16)
    score_ref[...] = jnp.broadcast_to(score, score_ref.shape)


def finish_kernel(history_ref, mine_ref, theirs_ref, right_ref, left_ref, out_ref, note_ref):
    acc = mine_ref[...].astype(F32) + theirs_ref[...].astype(F32)
    acc = (acc + right_ref[...].astype(F32)) + left_ref[...].astype(F32)
    out_ref[...] = acc
    peak = jnp.max(jnp.max(jnp.abs(acc), axis=0, keepdims=True), axis=1, keepdims=True)
    hist = history_ref[...]
    rest = jnp.broadcast_to(peak, (1, note_ref.shape[1] - hist.shape[1]))
    note_ref[...] = jnp.broadcast_to(jnp.concatenate([hist, rest], axis=1), note_ref.shape)


def scale_kernel(notes_ref, sum_ref, out_ref, history_ref):
    count = history_ref.shape[1]
    best = jnp.max(notes_ref[...], axis=0, keepdims=True)
    merged, peak = best[:, :count], best[:, count : count + 1]
    ref_amax = jnp.max(merged, axis=1, keepdims=True)
    scale = 1.0 / ref_amax
    out_ref[...] = sum_ref[...] * scale
    history_ref[...] = jnp.concatenate([merged[:, 1:], peak * scale * ref_amax], axis=1)


def whole(memory=pltpu.VMEM):
    return pl.BlockSpec(memory_space=memory)


def dispatch(routes, gates, grad, experts, cap, blocks):
    tokens, width = grad.shape
    block = pl.cdiv(width // blocks, LANES) * LANES
    rows = experts * cap
    return pl.pallas_call(
        functools.partial(dispatch_kernel, cap),
        out_shape=[
            jax.ShapeDtypeStruct((rows, width + LANES), BF16),
            jax.ShapeDtypeStruct((rows, tokens), BF16),
            jax.ShapeDtypeStruct((rows, tokens), BF16),
        ],
        in_specs=[whole(pl.ANY)] * 3,
        out_specs=[whole()] * 3,
        scratch_shapes=[
            pltpu.VMEM(routes.shape, routes.dtype),
            pltpu.VMEM(gates.shape, gates.dtype),
            pltpu.VMEM(grad.shape, grad.dtype),
            pltpu.VMEM((blocks, tokens, block), F32),
            pltpu.SemaphoreType.DMA((3,)),
        ],
        compiler_params=pltpu.CompilerParams(vmem_limit_bytes=16 << 20),
        name="dispatch",
    )(routes, gates, grad)


def gradients(rows, pre, weight, blocks):
    count = rows.shape[0]
    hidden, width = weight.shape
    tile = 256
    block = pl.cdiv(width // blocks, LANES) * LANES
    return pl.pallas_call(
        raw_kernel,
        grid=(count // tile,),
        out_shape=[
            jax.ShapeDtypeStruct(pre.shape, BF16),
            jax.ShapeDtypeStruct((count, LANES), F32),
        ],
        in_specs=[
            pl.BlockSpec((tile, rows.shape[1]), lambda i: (i, 0)),
            pl.BlockSpec((tile, pre.shape[1]), lambda i: (i, 0)),
            pl.BlockSpec((hidden, width), lambda i: (0, 0), pipeline_mode=pl.Buffered(1)),
        ],
        out_specs=[
            pl.BlockSpec((tile, pre.shape[1]), lambda i: (i, 0)),
            pl.BlockSpec((tile, LANES), lambda i: (i, 0)),
        ],
        scratch_shapes=[pltpu.VMEM((blocks, tile, block), F32)],
        compiler_params=pltpu.CompilerParams(vmem_limit_bytes=32 << 20),
        cost_estimate=pl.CostEstimate(
            flops=2 * count * hidden * width, bytes_accessed=12 << 20, transcendentals=0
        ),
        name="gradients",
    )(rows, pre, weight)


def finish(history, mine, theirs, right, left, n_ed):
    return pl.pallas_call(
        finish_kernel,
        out_shape=[
            jax.ShapeDtypeStruct(mine.shape, F32),
            jax.ShapeDtypeStruct((n_ed, LANES), F32),
        ],
        in_specs=[whole()] * 5,
        out_specs=[whole(), whole()],
        compiler_params=pltpu.CompilerParams(vmem_limit_bytes=16 << 20),
        name="finish",
    )(history, mine, theirs, right, left)


def scaled(notes, summed, count):
    return pl.pallas_call(
        scale_kernel,
        out_shape=[
            jax.ShapeDtypeStruct(summed.shape, F32),
            jax.ShapeDtypeStruct((1, count), F32),
        ],
        in_specs=[whole()] * 2,
        out_specs=[whole()] * 2,
        compiler_params=pltpu.CompilerParams(vmem_limit_bytes=16 << 20),
        name="scaled",
    )(notes, summed)


def tie(*values):
    return lax.optimization_barrier(values)


def swap(x, size):
    return lax.ppermute(x, "ed", [(i, i ^ 1) for i in range(size)])


def shift(x, by, size):
    return lax.ppermute(x, "ed", [(i, (i + 2 * by) % size) for i in range(size)])


def both(right, left, size):
    right, left = tie(right, left)
    return shift(right, 1, size), shift(left, -1, size)


def total(*terms):
    acc = terms[0].astype(F32)
    for term in terms[1:]:
        acc = acc + term.astype(F32)
    return acc.astype(BF16)


def body(out_grad, routes, gates, pre_acts, down_weight, history):
    n_src, cap = pre_acts.shape[2], pre_acts.shape[3]
    width_ff, width = down_weight.shape[1:]
    n_ep = lax.axis_size("ep")
    n_ed = lax.axis_size("ed")
    rows_in = n_src * cap
    rows = width // n_ed

    def exchange(x):
        moved = lax.all_to_all(
            x.reshape(n_ep, cap, x.shape[1]), "ep", split_axis=0, concat_axis=0, tiled=True
        )
        return moved.reshape(rows_in, x.shape[1])

    send, hot0, hot1 = dispatch(routes.T, gates.T, out_grad, n_ep, cap, n_ed)
    arrived = exchange(send)
    arrived, pre_acts, down_weight, history = tie(arrived, pre_acts, down_weight, history)

    pre_block = pre_acts[0, 0].reshape(rows_in, 2 * width_ff)
    gate_pre = pre_block[:, :width_ff].astype(F32)
    act = (gate_pre * jax.nn.sigmoid(gate_pre) * pre_block[:, width_ff:].astype(F32)).astype(BF16)
    gate_row = arrived[:, width : width + 1].astype(F32)
    weighted = lax.optimization_barrier((gate_row * act.astype(F32)).astype(BF16))

    half = n_ed // 4 * rows

    def term(index):
        return (
            jnp.einsum(
                "rd,rh->dh",
                arrived[:, index * half : (index + 1) * half],
                weighted,
                preferred_element_type=F32,
            )
            .astype(BF16)
            .reshape(n_ed // 4, rows, width_ff)
        )

    theirs_a = swap(term(0), n_ed)
    mine_a = term(2)
    cut = rows // 2
    start = total(mine_a[0], theirs_a[0])
    right, left = both(start[:cut], start[cut:], n_ed)
    theirs_b = swap(term(1), n_ed)
    mine_b = term(3)
    right, left, theirs_b, mine_b, arrived = tie(right, left, theirs_b, mine_b, arrived)

    right = jnp.pad(right, ((0, rows - cut), (0, 0)))
    left = jnp.pad(left, ((cut, 0), (0, 0)))
    right, left = both(
        total(mine_a[1], theirs_a[1], right), total(mine_a[2], theirs_a[2], left), n_ed
    )
    pre_grad, score = gradients(arrived, pre_block, down_weight[0], n_ed)
    right, left, score = tie(right, left, score)

    right, left = both(
        total(mine_a[3], theirs_a[3], right), total(mine_b[0], theirs_b[0], left), n_ed
    )
    returned = exchange(score)
    right, left, returned = tie(right, left, returned)
    right, left = both(
        total(mine_b[1], theirs_b[1], right), total(mine_b[2], theirs_b[2], left), n_ed
    )
    gate_grad = jnp.stack(
        [jnp.sum(hot0.astype(F32) * returned, axis=0), jnp.sum(hot1.astype(F32) * returned, axis=0)]
    ).T
    right, left, gate_grad = tie(right, left, gate_grad)

    summed, note = finish(history[0], mine_b[3], theirs_b[3], right, left, n_ed)
    notes = lax.all_to_all(note, "ed", split_axis=0, concat_axis=0, tiled=True)
    wgrad, new_history = scaled(notes, summed, history.shape[2])
    return (pre_grad.reshape(pre_acts.shape), wgrad[None], new_history, gate_grad)


def solution(mesh):
    placed = (
        P(("ed", "ep"), None),
        P(("ed", "ep"), None),
        P(("ed", "ep"), None),
        P("ed", "ep", None, None, None),
        P("ep", None, None),
        P("ed", "ep", None),
    )
    return jax.shard_map(
        body,
        mesh=mesh,
        in_specs=placed,
        out_specs=(
            P("ed", "ep", None, None, None),
            P("ep", "ed", None),
            P("ep", None),
            P(("ed", "ep"), None),
        ),
        check_vma=False,
    )
```

```python
import functools

import jax
import jax.numpy as jnp
from jax import lax
from jax.experimental import pallas as pl
from jax.experimental.pallas import tpu as pltpu
from jax.sharding import PartitionSpec as P

LANES = 128
BF16 = jnp.bfloat16
F32 = jnp.float32


def block_order(size):
    me = lax.axis_index("ed")
    place, core = me // 2, me % 2

    def listed(core):
        up = 1 - 2 * core

        def at(hops, which):
            return 2 * lax.rem(place + hops + size, size // 2) + which

        blocks = [at(4, core)]
        for hops in (3, 2, 1):
            blocks += [at(hops * up, 1 - core), at(hops * up, core)]
        return blocks + [at(0, core)]

    return listed(1 - core) + listed(core)


def dispatch_kernel(cap, routes_any, gates_any, grad_any, send_ref, hot0_ref, hot1_ref, routes_ref, gates_ref, grad_ref, held, sems):
    copies = [
        pltpu.make_async_copy(src, dst, sems.at[i])
        for i, (src, dst) in enumerate(
            [(routes_any, routes_ref), (gates_any, gates_ref), (grad_any, grad_ref)]
        )
    ]
    for copy in copies:
        copy.start()
    tokens, width = grad_ref.shape
    blocks = held.shape[0]
    block = width // blocks
    experts = send_ref.shape[0] // cap
    copies[0].wait()
    copies[1].wait()
    expert = lax.broadcasted_iota(jnp.int32, (experts, tokens), 0)
    one = routes_ref[0:1, :] == expert
    two = routes_ref[1:2, :] == expert
    named = jnp.where(one | two, 1.0, 0.0).astype(BF16)
    earlier = lax.broadcasted_iota(jnp.int32, (tokens, tokens), 0) < lax.broadcasted_iota(
        jnp.int32, (tokens, tokens), 1
    )
    before = jnp.dot(named, jnp.where(earlier, 1.0, 0.0).astype(BF16), preferred_element_type=F32)
    slots = lax.broadcasted_iota(jnp.int32, (experts, cap, tokens), 1)
    hit = slots == before.astype(jnp.int32)[:, None, :]
    gate0 = jnp.where(one, gates_ref[0:1, :].astype(F32), 0.0)
    gate1 = jnp.where(two, gates_ref[1:2, :].astype(F32), 0.0)
    rows = experts * cap
    hot0 = jnp.where(hit, jnp.where(one, 1.0, 0.0)[:, None, :], 0.0).reshape(rows, tokens)
    hot1 = jnp.where(hit, jnp.where(two, 1.0, 0.0)[:, None, :], 0.0).reshape(rows, tokens)
    gate = jnp.where(hit, (gate0 + gate1)[:, None, :], 0.0).reshape(rows, tokens)
    hot0_ref[...] = hot0.astype(BF16)
    hot1_ref[...] = hot1.astype(BF16)
    hot = (hot0 + hot1).astype(BF16)
    send_ref[:, width:] = jnp.dot(
        gate.astype(BF16), jnp.ones((tokens, LANES), BF16), preferred_element_type=F32
    ).astype(BF16)
    copies[2].wait()
    x = grad_ref[...].astype(F32)
    for b in range(blocks):
        held[b, :, :block] = x[:, b * block : (b + 1) * block]
    order = block_order(blocks)
    x = jnp.concatenate([held[i][:, :block] for i in order], axis=1).astype(BF16)
    send_ref[:, :width] = jnp.dot(hot, x, preferred_element_type=F32).astype(BF16)


def term_tiles(rows_ref, weighted, out_ref, first, block):
    step = 256
    flat = out_ref.shape[0] * block
    for c in range(0, flat, step):
        size = min(step, flat - c)
        tile = lax.dot_general(
            rows_ref[:, first + c : first + c + size],
            weighted,
            (((0,), (0,)), ((), ())),
            preferred_element_type=F32,
        ).astype(BF16)
        done = 0
        while done < size:
            i, j = divmod(c + done, block)
            count = min(block - j, size - done)
            out_ref[i, j : j + count, :] = tile[done : done + count]
            done += count


def first_terms_kernel(rows_ref, pre_ref, weighted_ref, theirs_ref, mine_ref):
    hidden = weighted_ref.shape[1]
    block = theirs_ref.shape[1]
    width = rows_ref.shape[1] - LANES
    gate = rows_ref[:, width:][:, :1].astype(F32)
    step = 256
    for n in range(0, hidden, step):
        gate_pre = pre_ref[:, n : n + step].astype(F32)
        act = gate_pre * jax.nn.sigmoid(gate_pre) * pre_ref[:, hidden + n : hidden + n + step].astype(F32)
        weighted_ref[:, n : n + step] = (gate * act.astype(BF16).astype(F32)).astype(BF16)
    weighted = weighted_ref[...]
    term_tiles(rows_ref, weighted, theirs_ref, 0, block)
    term_tiles(rows_ref, weighted, mine_ref, width // 2, block)


def more_terms_kernel(first, last, rows_ref, weighted_ref, theirs_ref, mine_ref):
    block = theirs_ref.shape[1]
    middle = (rows_ref.shape[1] - LANES) // 2
    weighted = weighted_ref[...]
    term_tiles(rows_ref, weighted, theirs_ref, first * block, block)
    term_tiles(rows_ref, weighted, mine_ref, middle + first * block, block)


def open_kernel(mine_ref, theirs_ref, one_ref, two_ref):
    for i, out_ref in enumerate((one_ref, two_ref)):
        out_ref[...] = (mine_ref[i].astype(F32) + theirs_ref[i].astype(F32)).astype(BF16)


def add_kernel(index, mine_ref, theirs_ref, moved_ref, out_ref):
    acc = mine_ref[index].astype(F32) + theirs_ref[index].astype(F32)
    out_ref[...] = (acc + moved_ref[...].astype(F32)).astype(BF16)


def raw_kernel(rows_ref, pre_ref, weight_ref, grad_ref, score_ref, held):
    hidden, width = weight_ref.shape
    blocks = held.shape[0]
    block = width // blocks
    tile = grad_ref.shape[0]
    here = pl.ds(pl.multiple_of(pl.program_id(0) * tile, tile), tile)
    x = rows_ref[here, :].astype(F32)
    for i, b in enumerate(block_order(blocks)):
        held[b, :, :block] = x[:, i * block : (i + 1) * block]
    rows = jnp.concatenate([held[b][:, :block] for b in range(blocks)], axis=1).astype(BF16)
    gate = x[:, width : width + 1]
    score = None
    step = 256
    for n in range(0, hidden, step):
        raw = lax.dot_general(
            rows, weight_ref[n : n + step, :], (((1,), (1,)), ((), ())), preferred_element_type=F32
        )
        gate_pre = pre_ref[here, n : n + step].astype(F32)
        up_pre = pre_ref[here, hidden + n : hidden + n + step].astype(F32)
        sigma = jax.nn.sigmoid(gate_pre)
        swish = gate_pre * sigma
        act = (swish * up_pre).astype(BF16).astype(F32)
        part = jnp.sum(act * raw, axis=1, keepdims=True)
        score = part if score is None else score + part
        grad_act = gate * raw
        grad_gate = grad_act * up_pre * sigma * (1.0 + gate_pre * (1.0 - sigma))
        grad_ref[:, n : n + step] = grad_gate.astype(BF16)
        grad_ref[:, hidden + n : hidden + n + step] = (grad_act * swish).astype(BF16)
    score_ref[...] = jnp.broadcast_to(score, score_ref.shape)


def finish_kernel(history_ref, mine_ref, theirs_ref, right_ref, left_ref, out_ref, note_ref):
    last = mine_ref.shape[0] - 1
    acc = mine_ref[last].astype(F32) + theirs_ref[last].astype(F32)
    acc = (acc + right_ref[...].astype(F32)) + left_ref[...].astype(F32)
    out_ref[...] = acc
    peak = jnp.max(jnp.max(jnp.abs(acc), axis=0, keepdims=True), axis=1, keepdims=True)
    hist = history_ref[...]
    rest = jnp.broadcast_to(peak, (1, note_ref.shape[1] - hist.shape[1]))
    note_ref[...] = jnp.broadcast_to(jnp.concatenate([hist, rest], axis=1), note_ref.shape)


def scale_kernel(notes_ref, sum_ref, out_ref, history_ref):
    count = history_ref.shape[1]
    best = jnp.max(notes_ref[...], axis=0, keepdims=True)
    merged, peak = best[:, :count], best[:, count : count + 1]
    ref_amax = jnp.max(merged, axis=1, keepdims=True)
    scale = 1.0 / ref_amax
    out_ref[...] = sum_ref[...] * scale
    history_ref[...] = jnp.concatenate([merged[:, 1:], peak * scale * ref_amax], axis=1)


def whole(memory=pltpu.VMEM):
    return pl.BlockSpec(memory_space=memory)


def dispatch(routes, gates, grad, experts, cap, blocks):
    tokens, width = grad.shape
    block = pl.cdiv(width // blocks, LANES) * LANES
    rows = experts * cap
    return pl.pallas_call(
        functools.partial(dispatch_kernel, cap),
        out_shape=[
            pltpu.VMEM((rows, width + LANES), BF16),
            pltpu.VMEM((rows, tokens), BF16),
            pltpu.VMEM((rows, tokens), BF16),
        ],
        in_specs=[whole(pltpu.HBM)] * 3,
        out_specs=[whole()] * 3,
        scratch_shapes=[
            pltpu.VMEM(routes.shape, routes.dtype),
            pltpu.VMEM(gates.shape, gates.dtype),
            pltpu.VMEM(grad.shape, grad.dtype),
            pltpu.VMEM((blocks, tokens, block), F32),
            pltpu.SemaphoreType.DMA((3,)),
        ],
        compiler_params=pltpu.CompilerParams(vmem_limit_bytes=16 << 20),
        name="dispatch",
    )(routes, gates, grad)


def gradients(rows, pre, weight, blocks):
    count = rows.shape[0]
    hidden, width = weight.shape
    tile = 256
    block = pl.cdiv(width // blocks, LANES) * LANES
    return pl.pallas_call(
        raw_kernel,
        grid=(count // tile,),
        out_shape=[
            jax.ShapeDtypeStruct(pre.shape, BF16),
            jax.ShapeDtypeStruct((count, LANES), F32),
        ],
        in_specs=[
            whole(),
            whole(),
            whole(),
        ],
        out_specs=[
            pl.BlockSpec((tile, pre.shape[1]), lambda i: (i, 0)),
            pl.BlockSpec((tile, LANES), lambda i: (i, 0)),
        ],
        scratch_shapes=[pltpu.VMEM((blocks, tile, block), F32)],
        compiler_params=pltpu.CompilerParams(vmem_limit_bytes=26 << 20),
        cost_estimate=SMALL,
        name="gradients",
    )(rows, pre, weight)


def finish(history, mine, theirs, right, left, n_ed):
    return pl.pallas_call(
        finish_kernel,
        out_shape=[
            pltpu.VMEM(right.shape, F32),
            pltpu.VMEM((n_ed, LANES), F32),
        ],
        in_specs=[whole()] * 5,
        out_specs=[whole(), whole()],
        compiler_params=pltpu.CompilerParams(vmem_limit_bytes=16 << 20),
        cost_estimate=SMALL,
        name="finish",
    )(history, mine, theirs, right, left)


def scaled(notes, summed, count):
    return pl.pallas_call(
        scale_kernel,
        out_shape=[
            jax.ShapeDtypeStruct(summed.shape, F32),
            jax.ShapeDtypeStruct((1, count), F32),
        ],
        in_specs=[whole()] * 2,
        out_specs=[whole()] * 2,
        compiler_params=pltpu.CompilerParams(vmem_limit_bytes=16 << 20),
        name="scaled",
    )(notes, summed)


LIMIT = 24 << 20
SMALL = pl.CostEstimate(flops=1 << 10, bytes_accessed=1 << 10, transcendentals=0)


def first_terms(rows, pre, block):
    hidden = pre.shape[1] // 2
    return pl.pallas_call(
        first_terms_kernel,
        out_shape=[pltpu.VMEM((rows.shape[0], hidden), BF16)]
        + [pltpu.VMEM((2, block, hidden), BF16)] * 2,
        in_specs=[whole()] * 2,
        out_specs=[whole()] * 3,
        compiler_params=pltpu.CompilerParams(vmem_limit_bytes=LIMIT),
        cost_estimate=SMALL,
        name="first_terms",
    )(rows, pre)


def more_terms(rows, weighted, first, last, block):
    hidden = weighted.shape[1]
    return pl.pallas_call(
        functools.partial(more_terms_kernel, first, last),
        out_shape=[pltpu.VMEM((last - first, block, hidden), BF16)] * 2,
        in_specs=[whole()] * 2,
        out_specs=[whole()] * 2,
        compiler_params=pltpu.CompilerParams(vmem_limit_bytes=LIMIT),
        cost_estimate=SMALL,
        name="more_terms",
    )(rows, weighted)


def open_sums(mine, theirs):
    return pl.pallas_call(
        open_kernel,
        out_shape=[pltpu.VMEM(mine.shape[1:], BF16)] * 2,
        in_specs=[whole()] * 2,
        out_specs=[whole()] * 2,
        compiler_params=pltpu.CompilerParams(vmem_limit_bytes=LIMIT),
        cost_estimate=SMALL,
        name="open_sums",
    )(mine, theirs)


def add(index, mine, theirs, moved):
    return pl.pallas_call(
        functools.partial(add_kernel, index),
        out_shape=pltpu.VMEM(moved.shape, BF16),
        in_specs=[whole()] * 3,
        out_specs=whole(),
        compiler_params=pltpu.CompilerParams(vmem_limit_bytes=LIMIT),
        cost_estimate=SMALL,
        name="add",
    )(mine, theirs, moved)


def tie(*values):
    return lax.optimization_barrier(values)


def swap(x, size):
    return lax.ppermute(x, "ed", [(i, i ^ 1) for i in range(size)])


def hop(x, size, cross=0):
    return lax.ppermute(
        x, "ed", [(i, ((i + 2 - 4 * (i % 2)) % size) ^ cross) for i in range(size)]
    )


def body(out_grad, routes, gates, pre_acts, down_weight, history):
    n_src, cap = pre_acts.shape[2], pre_acts.shape[3]
    width_ff, width = down_weight.shape[1:]
    n_ep = lax.axis_size("ep")
    n_ed = lax.axis_size("ed")
    rows_in = n_src * cap
    rows = width // n_ed

    def exchange(x):
        moved = lax.all_to_all(
            x.reshape(n_ep, cap, x.shape[1]), "ep", split_axis=0, concat_axis=0, tiled=True
        )
        return moved.reshape(rows_in, x.shape[1])

    send, hot0, hot1 = dispatch(
        *[
            pltpu.with_memory_space_constraint(x, pltpu.HBM)
            for x in (routes.T, gates.T, out_grad)
        ],
        n_ep,
        cap,
        n_ed,
    )
    arrived = exchange(send)
    arrived, pre_acts, down_weight, history = tie(arrived, pre_acts, down_weight, history)

    pre_block = pre_acts[0, 0].reshape(rows_in, 2 * width_ff)
    arrived, pre_block, weight = [
        pltpu.with_memory_space_constraint(x, pltpu.VMEM)
        for x in (arrived, pre_block, down_weight[0])
    ]
    weighted, theirs_e, mine_e = first_terms(arrived, pre_block, rows)
    theirs_e = swap(theirs_e, n_ed)
    theirs, mine = more_terms(arrived, weighted, 2, n_ed // 2, rows)
    theirs_e, theirs, mine = tie(theirs_e, theirs, mine)
    even, odd = open_sums(mine_e, theirs_e)
    even, odd, theirs, arrived = tie(even, odd, theirs, arrived)
    even, odd = hop(even, n_ed), hop(odd, n_ed)
    theirs = swap(theirs, n_ed)
    pre_grad, score = gradients(arrived, pre_block, weight, n_ed)
    even, theirs, mine, score = tie(even, theirs, mine, score)

    even = hop(add(0, mine, theirs, even), n_ed)
    odd = add(1, mine, theirs, odd)
    odd, score = tie(odd, score)
    odd = hop(odd, n_ed)
    returned = exchange(score)
    even, returned = tie(even, returned)

    even = hop(add(2, mine, theirs, even), n_ed)
    odd = hop(add(3, mine, theirs, odd), n_ed, 1)
    gate_grad = jnp.stack(
        [jnp.sum(hot0.astype(F32) * returned, axis=0), jnp.sum(hot1.astype(F32) * returned, axis=0)]
    ).T
    even, gate_grad = tie(even, gate_grad)
    even = hop(add(4, mine, theirs, even), n_ed)

    summed, note = finish(history[0], mine, theirs, even, odd, n_ed)
    notes = lax.all_to_all(note, "ed", split_axis=0, concat_axis=0, tiled=True)
    wgrad, new_history = scaled(notes, summed, history.shape[2])
    return (pre_grad.reshape(pre_acts.shape), wgrad[None], new_history, gate_grad)


def solution(mesh):
    placed = (
        P(("ed", "ep"), None),
        P(("ed", "ep"), None),
        P(("ed", "ep"), None),
        P("ed", "ep", None, None, None),
        P("ep", None, None),
        P("ed", "ep", None),
    )
    return jax.shard_map(
        body,
        mesh=mesh,
        in_specs=placed,
        out_specs=(
            P("ed", "ep", None, None, None),
            P("ep", "ed", None),
            P("ep", None),
            P(("ed", "ep"), None),
        ),
        check_vma=False,
    )
```

```python
import functools

import jax
import jax.numpy as jnp
from jax import lax
from jax.experimental import pallas as pl
from jax.experimental.pallas import tpu as pltpu
from jax.sharding import PartitionSpec as P

LANES = 128
BF16 = jnp.bfloat16
F32 = jnp.float32


def block_order(size):
    me = lax.axis_index("ed")
    place, core = me // 2, me % 2

    def listed(core):
        up = 1 - 2 * core

        def at(hops, which):
            return 2 * lax.rem(place + hops + size, size // 2) + which

        blocks = [at(4, core)]
        for hops in (3, 2, 1):
            blocks += [at(hops * up, 1 - core), at(hops * up, core)]
        return blocks + [at(0, core)]

    return listed(1 - core) + listed(core)


def dispatch_kernel(cap, routes_any, gates_any, grad_any, send_ref, inverse0_ref, inverse1_ref, routes_ref, gates_ref, grad_ref, held, sems):
    copies = [
        pltpu.make_async_copy(src, dst, sems.at[i])
        for i, (src, dst) in enumerate(
            [(routes_any, routes_ref), (gates_any, gates_ref), (grad_any, grad_ref)]
        )
    ]
    for copy in copies:
        copy.start()
    tokens, width = grad_ref.shape
    blocks = held.shape[0]
    block = width // blocks
    experts = send_ref.shape[0] // cap
    copies[0].wait()
    copies[1].wait()
    expert = lax.broadcasted_iota(jnp.int32, (experts, tokens), 0)
    one = routes_ref[0:1, :] == expert
    two = routes_ref[1:2, :] == expert
    named = jnp.where(one | two, 1.0, 0.0).astype(BF16)
    earlier = lax.broadcasted_iota(jnp.int32, (tokens, tokens), 0) < lax.broadcasted_iota(
        jnp.int32, (tokens, tokens), 1
    )
    before = jnp.dot(named, jnp.where(earlier, 1.0, 0.0).astype(BF16), preferred_element_type=F32)
    slots = lax.broadcasted_iota(jnp.int32, (experts, cap, tokens), 1)
    hit = slots == before.astype(jnp.int32)[:, None, :]
    gate0 = gates_ref[0:1, :].astype(F32)
    gate1 = gates_ref[1:2, :].astype(F32)
    rows = experts * cap

    def place(values):
        return jnp.where(hit, values[:, None, :], 0.0).reshape(rows, tokens)

    inverse0_ref[...] = place(jnp.where(one, 1.0 / gate0, 0.0))
    inverse1_ref[...] = place(jnp.where(two, 1.0 / gate1, 0.0))
    gate = place(jnp.where(one, gate0, 0.0) + jnp.where(two, gate1, 0.0)).astype(BF16)
    copies[2].wait()
    x = grad_ref[...]
    for b in range(blocks):
        held[b, :, :block] = x[:, b * block : (b + 1) * block]
    order = block_order(blocks)
    x = jnp.concatenate([held[i][:, :block] for i in order], axis=1)
    send_ref[...] = jnp.dot(gate, x, preferred_element_type=F32).astype(BF16)


def sigmoid(x):
    return 0.5 * jnp.tanh(0.5 * x) + 0.5


def term_tiles(rows_ref, weighted, out_ref, first, block):
    step = 256
    flat = out_ref.shape[0] * block
    for c in range(0, flat, step):
        size = min(step, flat - c)
        tile = lax.dot_general(
            rows_ref[:, first + c : first + c + size],
            weighted,
            (((0,), (0,)), ((), ())),
            preferred_element_type=F32,
        ).astype(BF16)
        done = 0
        while done < size:
            i, j = divmod(c + done, block)
            count = min(block - j, size - done)
            out_ref[i, j : j + count, :] = tile[done : done + count]
            done += count


def first_terms_kernel(rows_ref, pre_ref, act_ref, theirs_ref):
    hidden = act_ref.shape[1]
    step = 256
    for n in range(0, hidden, step):
        gate_pre = pre_ref[:, n : n + step].astype(F32)
        up_pre = pre_ref[:, hidden + n : hidden + n + step].astype(F32)
        act_ref[:, n : n + step] = (gate_pre * sigmoid(gate_pre) * up_pre).astype(BF16)
    term_tiles(rows_ref, act_ref[...], theirs_ref, 0, theirs_ref.shape[1])


def second_terms_kernel(rows_ref, act_ref, early_ref, theirs_ref, mine_ref):
    block = theirs_ref.shape[1]
    middle = rows_ref.shape[1] // 2
    act = act_ref[...]
    term_tiles(rows_ref, act, early_ref, middle, block)
    first = early_ref.shape[0] * block
    term_tiles(rows_ref, act, theirs_ref, first, block)
    term_tiles(rows_ref, act, mine_ref, middle + first, block)


def last_terms_kernel(first, rows_ref, act_ref, theirs_ref, mine_ref):
    block = theirs_ref.shape[1]
    middle = rows_ref.shape[1] // 2
    act = act_ref[...]
    term_tiles(rows_ref, act, theirs_ref, first * block, block)
    term_tiles(rows_ref, act, mine_ref, middle + first * block, block)


def open_kernel(mine_ref, theirs_ref, one_ref, two_ref):
    for i, out_ref in enumerate((one_ref, two_ref)):
        out_ref[...] = (mine_ref[i].astype(F32) + theirs_ref[i].astype(F32)).astype(BF16)


def add_kernel(index, mine_ref, theirs_ref, moved_ref, out_ref):
    acc = mine_ref[index].astype(F32) + theirs_ref[index].astype(F32)
    out_ref[...] = (acc + moved_ref[...].astype(F32)).astype(BF16)


def raw_kernel(rows_ref, pre_ref, weight_ref, grad_ref, score_ref, held):
    hidden, width = weight_ref.shape
    blocks = held.shape[0]
    block = width // blocks
    tile = grad_ref.shape[0]
    here = pl.ds(pl.multiple_of(pl.program_id(0) * tile, tile), tile)
    x = rows_ref[here, :]
    for i, b in enumerate(block_order(blocks)):
        held[b, :, :block] = x[:, i * block : (i + 1) * block]
    rows = jnp.concatenate([held[b][:, :block] for b in range(blocks)], axis=1)
    score = None
    step = 256
    for n in range(0, hidden, step):
        raw = lax.dot_general(
            rows, weight_ref[n : n + step, :], (((1,), (1,)), ((), ())), preferred_element_type=F32
        )
        gate_pre = pre_ref[here, n : n + step].astype(F32)
        up_pre = pre_ref[here, hidden + n : hidden + n + step].astype(F32)
        sigma = sigmoid(gate_pre)
        swish = gate_pre * sigma
        act = (swish * up_pre).astype(BF16).astype(F32)
        part = jnp.sum(act * raw, axis=1, keepdims=True)
        score = part if score is None else score + part
        slope = sigma + swish * (1.0 - sigma)
        grad_ref[:, n : n + step] = (raw * up_pre * slope).astype(BF16)
        grad_ref[:, hidden + n : hidden + n + step] = (raw * swish).astype(BF16)
    score_ref[...] = jnp.broadcast_to(score, score_ref.shape)


def finish_kernel(history_ref, mine_ref, theirs_ref, right_ref, left_ref, out_ref, note_ref):
    last = mine_ref.shape[0] - 1
    acc = mine_ref[last].astype(F32) + theirs_ref[last].astype(F32)
    acc = (acc + right_ref[...].astype(F32)) + left_ref[...].astype(F32)
    out_ref[...] = acc
    peak = jnp.max(jnp.max(jnp.abs(acc), axis=0, keepdims=True), axis=1, keepdims=True)
    hist = history_ref[...]
    rest = jnp.broadcast_to(peak, (1, note_ref.shape[1] - hist.shape[1]))
    note_ref[...] = jnp.broadcast_to(jnp.concatenate([hist, rest], axis=1), note_ref.shape)


def scale_kernel(notes_ref, sum_ref, out_ref, history_ref):
    count = history_ref.shape[1]
    best = jnp.max(notes_ref[...], axis=0, keepdims=True)
    merged, peak = best[:, :count], best[:, count : count + 1]
    ref_amax = jnp.max(merged, axis=1, keepdims=True)
    scale = 1.0 / ref_amax
    out_ref[...] = sum_ref[...] * scale
    history_ref[...] = jnp.concatenate([merged[:, 1:], peak * scale * ref_amax], axis=1)


def whole(memory=pltpu.VMEM):
    return pl.BlockSpec(memory_space=memory)


def dispatch(routes, gates, grad, experts, cap, blocks):
    tokens, width = grad.shape
    block = pl.cdiv(width // blocks, LANES) * LANES
    rows = experts * cap
    return pl.pallas_call(
        functools.partial(dispatch_kernel, cap),
        out_shape=[
            pltpu.VMEM((rows, width), BF16),
            pltpu.VMEM((rows, tokens), F32),
            pltpu.VMEM((rows, tokens), F32),
        ],
        in_specs=[whole(pltpu.HBM)] * 3,
        out_specs=[whole()] * 3,
        scratch_shapes=[
            pltpu.VMEM(routes.shape, routes.dtype),
            pltpu.VMEM(gates.shape, gates.dtype),
            pltpu.VMEM(grad.shape, grad.dtype),
            pltpu.VMEM((blocks, tokens, block), BF16),
            pltpu.SemaphoreType.DMA((3,)),
        ],
        compiler_params=pltpu.CompilerParams(vmem_limit_bytes=16 << 20),
        name="dispatch",
    )(routes, gates, grad)


def gradients(rows, pre, weight, blocks):
    count = rows.shape[0]
    hidden, width = weight.shape
    tile = 256
    block = pl.cdiv(width // blocks, LANES) * LANES
    return pl.pallas_call(
        raw_kernel,
        grid=(count // tile,),
        out_shape=[
            jax.ShapeDtypeStruct(pre.shape, BF16),
            jax.ShapeDtypeStruct((count, LANES), F32),
        ],
        in_specs=[
            whole(),
            whole(),
            whole(),
        ],
        out_specs=[
            pl.BlockSpec((tile, pre.shape[1]), lambda i: (i, 0)),
            pl.BlockSpec((tile, LANES), lambda i: (i, 0)),
        ],
        scratch_shapes=[pltpu.VMEM((blocks, tile, block), BF16)],
        compiler_params=pltpu.CompilerParams(vmem_limit_bytes=26 << 20),
        cost_estimate=SMALL,
        name="gradients",
    )(rows, pre, weight)


def finish(history, mine, theirs, right, left, n_ed):
    return pl.pallas_call(
        finish_kernel,
        out_shape=[
            pltpu.VMEM(right.shape, F32),
            pltpu.VMEM((n_ed, LANES), F32),
        ],
        in_specs=[whole()] * 5,
        out_specs=[whole(), whole()],
        compiler_params=pltpu.CompilerParams(vmem_limit_bytes=16 << 20),
        cost_estimate=SMALL,
        name="finish",
    )(history, mine, theirs, right, left)


def scaled(notes, summed, count):
    return pl.pallas_call(
        scale_kernel,
        out_shape=[
            jax.ShapeDtypeStruct(summed.shape, F32),
            jax.ShapeDtypeStruct((1, count), F32),
        ],
        in_specs=[whole()] * 2,
        out_specs=[whole()] * 2,
        compiler_params=pltpu.CompilerParams(vmem_limit_bytes=16 << 20),
        name="scaled",
    )(notes, summed)


LIMIT = 24 << 20
SMALL = pl.CostEstimate(flops=1 << 10, bytes_accessed=1 << 10, transcendentals=0)


def terms(kernel, name, counts, rows, other, block, act=None):
    hidden = (other if act is None else act).shape[1]
    if act is None:
        hidden = hidden // 2
    first = [pltpu.VMEM((rows.shape[0], hidden), BF16)] if act is None else []
    outs = first + [pltpu.VMEM((count, block, hidden), BF16) for count in counts]
    return pl.pallas_call(
        kernel,
        out_shape=outs,
        in_specs=[whole()] * 2,
        out_specs=[whole()] * len(outs),
        compiler_params=pltpu.CompilerParams(vmem_limit_bytes=LIMIT),
        cost_estimate=SMALL,
        name=name,
    )(rows, other if act is None else act)


def open_sums(mine, theirs):
    return pl.pallas_call(
        open_kernel,
        out_shape=[pltpu.VMEM(mine.shape[1:], BF16)] * 2,
        in_specs=[whole()] * 2,
        out_specs=[whole()] * 2,
        compiler_params=pltpu.CompilerParams(vmem_limit_bytes=LIMIT),
        cost_estimate=SMALL,
        name="open_sums",
    )(mine, theirs)


def add(index, mine, theirs, moved):
    return pl.pallas_call(
        functools.partial(add_kernel, index),
        out_shape=pltpu.VMEM(moved.shape, BF16),
        in_specs=[whole()] * 3,
        out_specs=whole(),
        compiler_params=pltpu.CompilerParams(vmem_limit_bytes=LIMIT),
        cost_estimate=SMALL,
        name="add",
    )(mine, theirs, moved)


def tie(*values):
    return lax.optimization_barrier(values)


def swap(x, size):
    return lax.ppermute(x, "ed", [(i, i ^ 1) for i in range(size)])


def hop(x, size, cross=0):
    return lax.ppermute(
        x, "ed", [(i, ((i + 2 - 4 * (i % 2)) % size) ^ cross) for i in range(size)]
    )


def body(out_grad, routes, gates, pre_acts, down_weight, history):
    n_src, cap = pre_acts.shape[2], pre_acts.shape[3]
    width_ff, width = down_weight.shape[1:]
    n_ep = lax.axis_size("ep")
    n_ed = lax.axis_size("ed")
    rows_in = n_src * cap
    rows = width // n_ed

    def exchange(x):
        moved = lax.all_to_all(
            x.reshape(n_ep, cap, x.shape[1]), "ep", split_axis=0, concat_axis=0, tiled=True
        )
        return moved.reshape(rows_in, x.shape[1])

    send, inverse0, inverse1 = dispatch(
        *[
            pltpu.with_memory_space_constraint(x, pltpu.HBM)
            for x in (routes.T, gates.T, out_grad)
        ],
        n_ep,
        cap,
        n_ed,
    )
    arrived = exchange(send)
    arrived, pre_acts, down_weight, history = tie(arrived, pre_acts, down_weight, history)

    pre_block = pre_acts[0, 0].reshape(rows_in, 2 * width_ff)
    arrived, pre_block, weight = [
        pltpu.with_memory_space_constraint(x, pltpu.VMEM)
        for x in (arrived, pre_block, down_weight[0])
    ]
    act, theirs_e = terms(first_terms_kernel, "first_terms", [2], arrived, pre_block, rows)
    theirs_e = swap(theirs_e, n_ed)
    mine_e, theirs_f, mine_f = terms(
        second_terms_kernel, "second_terms", [2, 2, 2], arrived, None, rows, act
    )
    theirs_e, mine_e, theirs_f, mine_f = tie(theirs_e, mine_e, theirs_f, mine_f)
    even, odd = open_sums(mine_e, theirs_e)
    even, odd, theirs_f, arrived, act = tie(even, odd, theirs_f, arrived, act)
    even, odd = hop(even, n_ed), hop(odd, n_ed)
    theirs_f = swap(theirs_f, n_ed)
    theirs, mine = terms(
        functools.partial(last_terms_kernel, 4), "last_terms", [4, 4], arrived, None, rows, act
    )
    theirs, mine, arrived = tie(theirs, mine, arrived)
    theirs = swap(theirs, n_ed)
    pre_grad, score = gradients(arrived, pre_block, weight, n_ed)
    even, theirs_f, mine, score = tie(even, theirs_f, mine, score)

    even = hop(add(0, mine_f, theirs_f, even), n_ed)
    odd = add(1, mine_f, theirs_f, odd)
    odd, score = tie(odd, score)
    odd = hop(odd, n_ed)
    returned = exchange(score)
    even, returned, theirs = tie(even, returned, theirs)

    even = hop(add(0, mine, theirs, even), n_ed)
    odd = hop(add(1, mine, theirs, odd), n_ed, 1)
    gate_grad = jnp.stack(
        [jnp.sum(inverse0 * returned, axis=0), jnp.sum(inverse1 * returned, axis=0)]
    ).T
    even, gate_grad = tie(even, gate_grad)
    even = hop(add(2, mine, theirs, even), n_ed)

    summed, note = finish(history[0], mine, theirs, even, odd, n_ed)
    notes = lax.all_to_all(note, "ed", split_axis=0, concat_axis=0, tiled=True)
    wgrad, new_history = scaled(notes, summed, history.shape[2])
    return (pre_grad.reshape(pre_acts.shape), wgrad[None], new_history, gate_grad)


def solution(mesh):
    placed = (
        P(("ed", "ep"), None),
        P(("ed", "ep"), None),
        P(("ed", "ep"), None),
        P("ed", "ep", None, None, None),
        P("ep", None, None),
        P("ed", "ep", None),
    )
    return jax.shard_map(
        body,
        mesh=mesh,
        in_specs=placed,
        out_specs=(
            P("ed", "ep", None, None, None),
            P("ep", "ed", None),
            P("ep", None),
            P(("ed", "ep"), None),
        ),
        check_vma=False,
    )
```

```python
import functools

import jax
import jax.numpy as jnp
from jax import lax
from jax.experimental import pallas as pl
from jax.experimental.pallas import tpu as pltpu
from jax.sharding import PartitionSpec as P

LANES = 128
BF16 = jnp.bfloat16
F32 = jnp.float32


def block_order(size):
    me = lax.axis_index("ed")
    place, core = me // 2, me % 2

    def listed(core):
        up = 1 - 2 * core

        def at(hops, which):
            return 2 * lax.rem(place + hops + size, size // 2) + which

        blocks = [at(4, core)]
        for hops in (3, 2, 1):
            blocks += [at(hops * up, 1 - core), at(hops * up, core)]
        return blocks + [at(0, core)]

    return listed(1 - core) + listed(core)


def dispatch_kernel(cap, routes_any, gates_any, grad_any, send_ref, inverse0_ref, inverse1_ref, routes_ref, gates_ref, grad_ref, held, sems):
    copies = [
        pltpu.make_async_copy(src, dst, sems.at[i])
        for i, (src, dst) in enumerate(
            [(routes_any, routes_ref), (gates_any, gates_ref), (grad_any, grad_ref)]
        )
    ]
    for copy in copies:
        copy.start()
    tokens, width = grad_ref.shape
    blocks = held.shape[0]
    block = width // blocks
    experts = send_ref.shape[0] // cap
    copies[0].wait()
    copies[1].wait()
    expert = lax.broadcasted_iota(jnp.int32, (experts, tokens), 0)
    one = routes_ref[0:1, :] == expert
    two = routes_ref[1:2, :] == expert
    named = jnp.where(one | two, 1.0, 0.0).astype(BF16)
    earlier = lax.broadcasted_iota(jnp.int32, (tokens, tokens), 0) < lax.broadcasted_iota(
        jnp.int32, (tokens, tokens), 1
    )
    before = jnp.dot(named, jnp.where(earlier, 1.0, 0.0).astype(BF16), preferred_element_type=F32)
    slots = lax.broadcasted_iota(jnp.int32, (experts, cap, tokens), 1)
    hit = slots == before.astype(jnp.int32)[:, None, :]
    gate0 = gates_ref[0:1, :].astype(F32)
    gate1 = gates_ref[1:2, :].astype(F32)
    rows = experts * cap

    def place(values):
        return jnp.where(hit, values[:, None, :], 0.0).reshape(rows, tokens)

    inverse0_ref[...] = place(jnp.where(one, 1.0 / gate0, 0.0))
    inverse1_ref[...] = place(jnp.where(two, 1.0 / gate1, 0.0))
    gate = place(jnp.where(one, gate0, 0.0) + jnp.where(two, gate1, 0.0)).astype(BF16)
    copies[2].wait()
    x = grad_ref[...]
    for b in range(blocks):
        held[b, :, :block] = x[:, b * block : (b + 1) * block]
    order = block_order(blocks)
    x = jnp.concatenate([held[i][:, :block] for i in order], axis=1)
    send_ref[...] = jnp.dot(gate, x, preferred_element_type=F32).astype(BF16)


def sigmoid(x):
    return 0.5 * jnp.tanh(0.5 * x) + 0.5


def term_tiles(rows_ref, weighted, out_ref, first, block):
    step = 256
    flat = out_ref.shape[0] * block
    for c in range(0, flat, step):
        size = min(step, flat - c)
        tile = lax.dot_general(
            rows_ref[:, first + c : first + c + size],
            weighted,
            (((0,), (0,)), ((), ())),
            preferred_element_type=F32,
        ).astype(BF16)
        done = 0
        while done < size:
            i, j = divmod(c + done, block)
            count = min(block - j, size - done)
            out_ref[i, j : j + count, :] = tile[done : done + count]
            done += count


def first_terms_kernel(rows_ref, pre_ref, act_ref, theirs_ref):
    hidden = act_ref.shape[1]
    step = 256
    for n in range(0, hidden, step):
        gate_pre = pre_ref[:, n : n + step].astype(F32)
        up_pre = pre_ref[:, hidden + n : hidden + n + step].astype(F32)
        act_ref[:, n : n + step] = (gate_pre * sigmoid(gate_pre) * up_pre).astype(BF16)
    term_tiles(rows_ref, act_ref[...], theirs_ref, 0, theirs_ref.shape[1])


def second_terms_kernel(rows_ref, act_ref, early_ref, theirs_ref, mine_ref):
    block = theirs_ref.shape[1]
    middle = rows_ref.shape[1] // 2
    act = act_ref[...]
    term_tiles(rows_ref, act, early_ref, middle, block)
    first = early_ref.shape[0] * block
    term_tiles(rows_ref, act, theirs_ref, first, block)
    term_tiles(rows_ref, act, mine_ref, middle + first, block)


def last_terms_kernel(first, rows_ref, act_ref, theirs_ref, mine_ref):
    block = theirs_ref.shape[1]
    middle = rows_ref.shape[1] // 2
    act = act_ref[...]
    term_tiles(rows_ref, act, theirs_ref, first * block, block)
    term_tiles(rows_ref, act, mine_ref, middle + first * block, block)


def open_kernel(mine_ref, theirs_ref, one_ref, two_ref):
    for i, out_ref in enumerate((one_ref, two_ref)):
        out_ref[...] = (mine_ref[i].astype(F32) + theirs_ref[i].astype(F32)).astype(BF16)


def add_kernel(index, mine_ref, theirs_ref, moved_ref, out_ref):
    acc = mine_ref[index].astype(F32) + theirs_ref[index].astype(F32)
    out_ref[...] = (acc + moved_ref[...].astype(F32)).astype(BF16)


def raw_kernel(rows_ref, pre_ref, weight_ref, grad_ref, score_ref, held):
    hidden, width = weight_ref.shape
    blocks = held.shape[0]
    block = width // blocks
    tile = grad_ref.shape[0]
    here = pl.ds(pl.multiple_of(pl.program_id(0) * tile, tile), tile)
    x = rows_ref[here, :]
    for i, b in enumerate(block_order(blocks)):
        held[b, :, :block] = x[:, i * block : (i + 1) * block]
    rows = jnp.concatenate([held[b][:, :block] for b in range(blocks)], axis=1)
    score = None
    step = 256
    for n in range(0, hidden, step):
        raw = lax.dot_general(
            rows, weight_ref[n : n + step, :], (((1,), (1,)), ((), ())), preferred_element_type=F32
        )
        gate_pre = pre_ref[here, n : n + step].astype(F32)
        up_pre = pre_ref[here, hidden + n : hidden + n + step].astype(F32)
        sigma = sigmoid(gate_pre)
        swish = gate_pre * sigma
        act = (swish * up_pre).astype(BF16).astype(F32)
        part = jnp.sum(act * raw, axis=1, keepdims=True)
        score = part if score is None else score + part
        slope = sigma + swish * (1.0 - sigma)
        grad_ref[:, n : n + step] = (raw * up_pre * slope).astype(BF16)
        grad_ref[:, hidden + n : hidden + n + step] = (raw * swish).astype(BF16)
    score_ref[...] = jnp.broadcast_to(score, score_ref.shape)


def finish_kernel(history_ref, mine_ref, theirs_ref, right_ref, left_ref, out_ref, note_ref):
    last = mine_ref.shape[0] - 1
    acc = mine_ref[last].astype(F32) + theirs_ref[last].astype(F32)
    acc = (acc + right_ref[...].astype(F32)) + left_ref[...].astype(F32)
    out_ref[...] = acc
    peak = jnp.max(jnp.max(jnp.abs(acc), axis=0, keepdims=True), axis=1, keepdims=True)
    hist = history_ref[...]
    rest = jnp.broadcast_to(peak, (1, note_ref.shape[1] - hist.shape[1]))
    note_ref[...] = jnp.broadcast_to(jnp.concatenate([hist, rest], axis=1), note_ref.shape)


def scale_kernel(notes_ref, sum_ref, out_ref, history_ref):
    count = history_ref.shape[1]
    best = jnp.max(notes_ref[...], axis=0, keepdims=True)
    merged, peak = best[:, :count], best[:, count : count + 1]
    ref_amax = jnp.max(merged, axis=1, keepdims=True)
    scale = 1.0 / ref_amax
    out_ref[...] = sum_ref[...] * scale
    history_ref[...] = jnp.concatenate([merged[:, 1:], peak * scale * ref_amax], axis=1)


def whole(memory=pltpu.VMEM):
    return pl.BlockSpec(memory_space=memory)


def dispatch(routes, gates, grad, experts, cap, blocks):
    tokens, width = grad.shape
    block = pl.cdiv(width // blocks, LANES) * LANES
    rows = experts * cap
    return pl.pallas_call(
        functools.partial(dispatch_kernel, cap),
        out_shape=[
            pltpu.VMEM((rows, width), BF16),
            pltpu.VMEM((rows, tokens), F32),
            pltpu.VMEM((rows, tokens), F32),
        ],
        in_specs=[whole(pltpu.HBM)] * 3,
        out_specs=[whole()] * 3,
        scratch_shapes=[
            pltpu.VMEM(routes.shape, routes.dtype),
            pltpu.VMEM(gates.shape, gates.dtype),
            pltpu.VMEM(grad.shape, grad.dtype),
            pltpu.VMEM((blocks, tokens, block), BF16),
            pltpu.SemaphoreType.DMA((3,)),
        ],
        compiler_params=pltpu.CompilerParams(vmem_limit_bytes=16 << 20),
        name="dispatch",
    )(routes, gates, grad)


def gradients(rows, pre, weight, blocks):
    count = rows.shape[0]
    hidden, width = weight.shape
    tile = 256
    block = pl.cdiv(width // blocks, LANES) * LANES
    return pl.pallas_call(
        raw_kernel,
        grid=(count // tile,),
        out_shape=[
            jax.ShapeDtypeStruct(pre.shape, BF16),
            jax.ShapeDtypeStruct((count, LANES), F32),
        ],
        in_specs=[
            whole(),
            whole(),
            whole(),
        ],
        out_specs=[
            pl.BlockSpec((tile, pre.shape[1]), lambda i: (i, 0)),
            pl.BlockSpec((tile, LANES), lambda i: (i, 0)),
        ],
        scratch_shapes=[pltpu.VMEM((blocks, tile, block), BF16)],
        compiler_params=pltpu.CompilerParams(vmem_limit_bytes=26 << 20),
        cost_estimate=SMALL,
        name="gradients",
    )(rows, pre, weight)


def finish(history, mine, theirs, right, left, n_ed):
    return pl.pallas_call(
        finish_kernel,
        out_shape=[
            pltpu.VMEM(right.shape, F32),
            pltpu.VMEM((n_ed, LANES), F32),
        ],
        in_specs=[whole()] * 5,
        out_specs=[whole(), whole()],
        compiler_params=pltpu.CompilerParams(vmem_limit_bytes=16 << 20),
        cost_estimate=SMALL,
        name="finish",
    )(history, mine, theirs, right, left)


def scaled(notes, summed, count):
    return pl.pallas_call(
        scale_kernel,
        out_shape=[
            jax.ShapeDtypeStruct(summed.shape, F32),
            jax.ShapeDtypeStruct((1, count), F32),
        ],
        in_specs=[whole()] * 2,
        out_specs=[whole()] * 2,
        compiler_params=pltpu.CompilerParams(vmem_limit_bytes=16 << 20),
        name="scaled",
    )(notes, summed)


LIMIT = 24 << 20
SMALL = pl.CostEstimate(flops=1 << 10, bytes_accessed=1 << 10, transcendentals=0)


def terms(kernel, name, counts, rows, other, block, act=None):
    hidden = (other if act is None else act).shape[1]
    if act is None:
        hidden = hidden // 2
    first = [pltpu.VMEM((rows.shape[0], hidden), BF16)] if act is None else []
    outs = first + [pltpu.VMEM((count, block, hidden), BF16) for count in counts]
    return pl.pallas_call(
        kernel,
        out_shape=outs,
        in_specs=[whole()] * 2,
        out_specs=[whole()] * len(outs),
        compiler_params=pltpu.CompilerParams(vmem_limit_bytes=LIMIT),
        cost_estimate=SMALL,
        name=name,
    )(rows, other if act is None else act)


def open_sums(mine, theirs):
    return pl.pallas_call(
        open_kernel,
        out_shape=[pltpu.VMEM(mine.shape[1:], BF16)] * 2,
        in_specs=[whole()] * 2,
        out_specs=[whole()] * 2,
        compiler_params=pltpu.CompilerParams(vmem_limit_bytes=LIMIT),
        cost_estimate=SMALL,
        name="open_sums",
    )(mine, theirs)


def add(index, mine, theirs, moved):
    return pl.pallas_call(
        functools.partial(add_kernel, index),
        out_shape=pltpu.VMEM(moved.shape, BF16),
        in_specs=[whole()] * 3,
        out_specs=whole(),
        compiler_params=pltpu.CompilerParams(vmem_limit_bytes=LIMIT),
        cost_estimate=SMALL,
        name="add",
    )(mine, theirs, moved)


def tie(*values):
    return lax.optimization_barrier(values)


def swap(x, size):
    return lax.ppermute(x, "ed", [(i, i ^ 1) for i in range(size)])


def hop(x, size, cross=0):
    return lax.ppermute(
        x, "ed", [(i, ((i + 2 - 4 * (i % 2)) % size) ^ cross) for i in range(size)]
    )


def body(out_grad, routes, gates, pre_acts, down_weight, history):
    n_src, cap = pre_acts.shape[2], pre_acts.shape[3]
    width_ff, width = down_weight.shape[1:]
    n_ep = lax.axis_size("ep")
    n_ed = lax.axis_size("ed")
    rows_in = n_src * cap
    rows = width // n_ed

    def exchange(x):
        moved = lax.all_to_all(
            x.reshape(n_ep, cap, x.shape[1]), "ep", split_axis=0, concat_axis=0, tiled=True
        )
        return moved.reshape(rows_in, x.shape[1])

    send, inverse0, inverse1 = dispatch(
        *[
            pltpu.with_memory_space_constraint(x, pltpu.HBM)
            for x in (routes.T, gates.T, out_grad)
        ],
        n_ep,
        cap,
        n_ed,
    )
    arrived = exchange(send)
    arrived, pre_acts, down_weight, history = tie(arrived, pre_acts, down_weight, history)

    pre_block = pre_acts[0, 0].reshape(rows_in, 2 * width_ff)
    arrived, pre_block, weight = [
        pltpu.with_memory_space_constraint(x, pltpu.VMEM)
        for x in (arrived, pre_block, down_weight[0])
    ]
    act, theirs_e = terms(first_terms_kernel, "first_terms", [2], arrived, pre_block, rows)
    theirs_e = swap(theirs_e, n_ed)
    mine_e, theirs_f, mine_f = terms(
        second_terms_kernel, "second_terms", [2, 2, 2], arrived, None, rows, act
    )
    theirs_e, mine_e, theirs_f, mine_f = tie(theirs_e, mine_e, theirs_f, mine_f)
    even, odd = open_sums(mine_e, theirs_e)
    even, odd, theirs_f, arrived, act = tie(even, odd, theirs_f, arrived, act)
    even, odd = hop(even, n_ed), hop(odd, n_ed)
    theirs_f = swap(theirs_f, n_ed)
    theirs, mine = terms(
        functools.partial(last_terms_kernel, 4), "last_terms", [4, 4], arrived, None, rows, act
    )
    theirs, mine, arrived = tie(theirs, mine, arrived)
    theirs = swap(theirs, n_ed)
    pre_grad, score = gradients(arrived, pre_block, weight, n_ed)
    even, theirs_f, mine, score = tie(even, theirs_f, mine, score)

    even = hop(add(0, mine_f, theirs_f, even), n_ed)
    odd = add(1, mine_f, theirs_f, odd)
    odd, score = tie(odd, score)
    odd = hop(odd, n_ed)
    returned = exchange(score)
    even, returned, theirs = tie(even, returned, theirs)

    even = hop(add(0, mine, theirs, even), n_ed)
    odd = hop(add(1, mine, theirs, odd), n_ed, 1)
    gate_grad = jnp.stack(
        [jnp.sum(inverse0 * returned, axis=0), jnp.sum(inverse1 * returned, axis=0)]
    ).T
    even, gate_grad = tie(even, gate_grad)
    even = hop(add(2, mine, theirs, even), n_ed)

    summed, note = finish(history[0], mine, theirs, even, odd, n_ed)
    high, low = range(n_ed // 4, n_ed // 2), range(n_ed // 4)
    listed = [2 * place + core for core in (1, 0) for place in (*high, *low)]
    notes = lax.all_to_all(
        note,
        "ed",
        split_axis=0,
        concat_axis=0,
        tiled=True,
        axis_index_groups=[listed],
    )
    wgrad, new_history = scaled(notes, summed, history.shape[2])
    return (pre_grad.reshape(pre_acts.shape), wgrad[None], new_history, gate_grad)


def solution(mesh):
    placed = (
        P(("ed", "ep"), None),
        P(("ed", "ep"), None),
        P(("ed", "ep"), None),
        P("ed", "ep", None, None, None),
        P("ep", None, None),
        P("ed", "ep", None),
    )
    return jax.shard_map(
        body,
        mesh=mesh,
        in_specs=placed,
        out_specs=(
            P("ed", "ep", None, None, None),
            P("ep", "ed", None),
            P("ep", None),
            P(("ed", "ep"), None),
        ),
        check_vma=False,
    )
```

```python
import functools

import jax
import jax.numpy as jnp
from jax import lax
from jax.experimental import pallas as pl
from jax.experimental.pallas import tpu as pltpu
from jax.sharding import PartitionSpec as P

LANES = 128
BF16 = jnp.bfloat16
F32 = jnp.float32


def block_order(size):
    me = lax.axis_index("ed")
    place, core = me // 2, me % 2

    def listed(core):
        up = 1 - 2 * core

        def at(hops, which):
            return 2 * lax.rem(place + hops + size, size // 2) + which

        blocks = [at(4, core)]
        for hops in (3, 2, 1):
            blocks += [at(hops * up, 1 - core), at(hops * up, core)]
        return blocks + [at(0, core)]

    return listed(1 - core) + listed(core)


def dispatch_kernel(cap, routes_any, gates_any, grad_any, send_ref, inverse0_ref, inverse1_ref, routes_ref, gates_ref, grad_ref, held, sems):
    copies = [
        pltpu.make_async_copy(src, dst, sems.at[i])
        for i, (src, dst) in enumerate(
            [(routes_any, routes_ref), (gates_any, gates_ref), (grad_any, grad_ref)]
        )
    ]
    for copy in copies:
        copy.start()
    tokens, width = grad_ref.shape
    blocks = held.shape[0]
    block = width // blocks
    experts = send_ref.shape[0] // cap
    copies[0].wait()
    copies[1].wait()
    expert = lax.broadcasted_iota(jnp.int32, (experts, tokens), 0)
    one = routes_ref[0:1, :] == expert
    two = routes_ref[1:2, :] == expert
    named = jnp.where(one | two, 1.0, 0.0).astype(BF16)
    earlier = lax.broadcasted_iota(jnp.int32, (tokens, tokens), 0) < lax.broadcasted_iota(
        jnp.int32, (tokens, tokens), 1
    )
    before = jnp.dot(named, jnp.where(earlier, 1.0, 0.0).astype(BF16), preferred_element_type=F32)
    slots = lax.broadcasted_iota(jnp.int32, (experts, cap, tokens), 1)
    hit = slots == before.astype(jnp.int32)[:, None, :]
    gate0 = gates_ref[0:1, :].astype(F32)
    gate1 = gates_ref[1:2, :].astype(F32)
    rows = experts * cap

    def place(values):
        return jnp.where(hit, values[:, None, :], 0.0).reshape(rows, tokens)

    inverse0_ref[...] = place(jnp.where(one, 1.0 / gate0, 0.0))
    inverse1_ref[...] = place(jnp.where(two, 1.0 / gate1, 0.0))
    gate = place(jnp.where(one, gate0, 0.0) + jnp.where(two, gate1, 0.0)).astype(BF16)
    copies[2].wait()
    x = grad_ref[...]
    for b in range(blocks):
        held[b, :, :block] = x[:, b * block : (b + 1) * block]
    order = block_order(blocks)
    x = jnp.concatenate([held[i][:, :block] for i in order], axis=1)
    send_ref[...] = jnp.dot(gate, x, preferred_element_type=F32).astype(BF16)


def sigmoid(x):
    return 0.5 * jnp.tanh(0.5 * x) + 0.5


def term_tiles(rows_ref, weighted, out_ref, first, block):
    step = 256
    flat = out_ref.shape[0] * block
    for c in range(0, flat, step):
        size = min(step, flat - c)
        tile = lax.dot_general(
            rows_ref[:, first + c : first + c + size],
            weighted,
            (((0,), (0,)), ((), ())),
            preferred_element_type=F32,
        ).astype(BF16)
        done = 0
        while done < size:
            i, j = divmod(c + done, block)
            count = min(block - j, size - done)
            out_ref[i, j : j + count, :] = tile[done : done + count]
            done += count


def first_terms_kernel(rows_ref, pre_ref, act_ref, theirs_ref):
    hidden = act_ref.shape[1]
    step = 256
    for n in range(0, hidden, step):
        gate_pre = pre_ref[:, n : n + step].astype(F32)
        up_pre = pre_ref[:, hidden + n : hidden + n + step].astype(F32)
        act_ref[:, n : n + step] = (gate_pre * sigmoid(gate_pre) * up_pre).astype(BF16)
    term_tiles(rows_ref, act_ref[...], theirs_ref, 0, theirs_ref.shape[1])


def second_terms_kernel(rows_ref, act_ref, early_ref, theirs_ref, mine_ref):
    block = theirs_ref.shape[1]
    middle = rows_ref.shape[1] // 2
    act = act_ref[...]
    term_tiles(rows_ref, act, early_ref, middle, block)
    first = early_ref.shape[0] * block
    term_tiles(rows_ref, act, theirs_ref, first, block)
    term_tiles(rows_ref, act, mine_ref, middle + first, block)


def last_terms_kernel(first, rows_ref, act_ref, theirs_ref, mine_ref):
    block = theirs_ref.shape[1]
    middle = rows_ref.shape[1] // 2
    act = act_ref[...]
    term_tiles(rows_ref, act, theirs_ref, first * block, block)
    term_tiles(rows_ref, act, mine_ref, middle + first * block, block)


def open_kernel(mine_ref, theirs_ref, one_ref, two_ref):
    for i, out_ref in enumerate((one_ref, two_ref)):
        out_ref[...] = (mine_ref[i].astype(F32) + theirs_ref[i].astype(F32)).astype(BF16)


def add_kernel(index, mine_ref, theirs_ref, moved_ref, out_ref):
    acc = mine_ref[index].astype(F32) + theirs_ref[index].astype(F32)
    out_ref[...] = (acc + moved_ref[...].astype(F32)).astype(BF16)


def raw_kernel(rows_ref, pre_ref, weight_ref, grad_ref, score_ref, held):
    hidden, width = weight_ref.shape
    blocks = held.shape[0]
    block = width // blocks
    tile = grad_ref.shape[0]
    here = pl.ds(pl.multiple_of(pl.program_id(0) * tile, tile), tile)
    x = rows_ref[here, :]
    for i, b in enumerate(block_order(blocks)):
        held[b, :, :block] = x[:, i * block : (i + 1) * block]
    rows = jnp.concatenate([held[b][:, :block] for b in range(blocks)], axis=1)
    score = None
    step = 256
    for n in range(0, hidden, step):
        raw = lax.dot_general(
            rows, weight_ref[n : n + step, :], (((1,), (1,)), ((), ())), preferred_element_type=F32
        )
        gate_pre = pre_ref[here, n : n + step].astype(F32)
        up_pre = pre_ref[here, hidden + n : hidden + n + step].astype(F32)
        sigma = sigmoid(gate_pre)
        swish = gate_pre * sigma
        act = (swish * up_pre).astype(BF16).astype(F32)
        part = jnp.sum(act * raw, axis=1, keepdims=True)
        score = part if score is None else score + part
        slope = sigma + swish * (1.0 - sigma)
        grad_ref[:, n : n + step] = (raw * up_pre * slope).astype(BF16)
        grad_ref[:, hidden + n : hidden + n + step] = (raw * swish).astype(BF16)
    score_ref[...] = jnp.broadcast_to(score, score_ref.shape)


def finish_kernel(history_ref, mine_ref, theirs_ref, right_ref, left_ref, out_ref, note_ref):
    last = mine_ref.shape[0] - 1
    acc = mine_ref[last].astype(F32) + theirs_ref[last].astype(F32)
    acc = (acc + right_ref[...].astype(F32)) + left_ref[...].astype(F32)
    out_ref[...] = acc
    peak = jnp.max(jnp.max(jnp.abs(acc), axis=0, keepdims=True), axis=1, keepdims=True)
    hist = history_ref[...]
    rest = jnp.broadcast_to(peak, (1, note_ref.shape[1] - hist.shape[1]))
    note_ref[...] = jnp.broadcast_to(jnp.concatenate([hist, rest], axis=1), note_ref.shape)


def scale_kernel(notes_ref, sum_ref, out_ref, history_ref):
    count = history_ref.shape[1]
    best = jnp.max(notes_ref[...], axis=0, keepdims=True)
    merged, peak = best[:, :count], best[:, count : count + 1]
    ref_amax = jnp.max(merged, axis=1, keepdims=True)
    scale = 1.0 / ref_amax
    tile = out_ref.shape[0]
    here = pl.ds(pl.multiple_of(pl.program_id(0) * tile, tile), tile)
    out_ref[...] = sum_ref[here, :] * scale
    history_ref[...] = jnp.concatenate([merged[:, 1:], peak * scale * ref_amax], axis=1)


def whole(memory=pltpu.VMEM):
    return pl.BlockSpec(memory_space=memory)


def dispatch(routes, gates, grad, experts, cap, blocks):
    tokens, width = grad.shape
    block = pl.cdiv(width // blocks, LANES) * LANES
    rows = experts * cap
    return pl.pallas_call(
        functools.partial(dispatch_kernel, cap),
        out_shape=[
            pltpu.VMEM((rows, width), BF16),
            pltpu.VMEM((rows, tokens), F32),
            pltpu.VMEM((rows, tokens), F32),
        ],
        in_specs=[whole(pltpu.HBM)] * 3,
        out_specs=[whole()] * 3,
        scratch_shapes=[
            pltpu.VMEM(routes.shape, routes.dtype),
            pltpu.VMEM(gates.shape, gates.dtype),
            pltpu.VMEM(grad.shape, grad.dtype),
            pltpu.VMEM((blocks, tokens, block), BF16),
            pltpu.SemaphoreType.DMA((3,)),
        ],
        compiler_params=pltpu.CompilerParams(vmem_limit_bytes=16 << 20),
        name="dispatch",
    )(routes, gates, grad)


def gradients(rows, pre, weight, blocks):
    count = rows.shape[0]
    hidden, width = weight.shape
    tile = 256
    block = pl.cdiv(width // blocks, LANES) * LANES
    return pl.pallas_call(
        raw_kernel,
        grid=(count // tile,),
        out_shape=[
            jax.ShapeDtypeStruct(pre.shape, BF16),
            jax.ShapeDtypeStruct((count, LANES), F32),
        ],
        in_specs=[
            whole(),
            whole(),
            whole(),
        ],
        out_specs=[
            pl.BlockSpec((tile, pre.shape[1]), lambda i: (i, 0)),
            pl.BlockSpec((tile, LANES), lambda i: (count // tile - 1 - i, 0)),
        ],
        scratch_shapes=[pltpu.VMEM((blocks, tile, block), BF16)],
        compiler_params=pltpu.CompilerParams(vmem_limit_bytes=26 << 20),
        cost_estimate=SMALL,
        name="gradients",
    )(rows, pre, weight)


def finish(history, mine, theirs, right, left, n_ed):
    return pl.pallas_call(
        finish_kernel,
        out_shape=[
            pltpu.VMEM(right.shape, F32),
            pltpu.VMEM((n_ed, LANES), F32),
        ],
        in_specs=[whole()] * 5,
        out_specs=[whole(), whole()],
        compiler_params=pltpu.CompilerParams(vmem_limit_bytes=16 << 20),
        cost_estimate=SMALL,
        name="finish",
    )(history, mine, theirs, right, left)


def scaled(notes, summed, count):
    return pl.pallas_call(
        scale_kernel,
        grid=(4,),
        out_shape=[
            jax.ShapeDtypeStruct(summed.shape, F32),
            jax.ShapeDtypeStruct((1, count), F32),
        ],
        in_specs=[whole()] * 2,
        out_specs=[
            pl.BlockSpec((summed.shape[0] // 4, summed.shape[1]), lambda i: (i, 0)),
            pl.BlockSpec((1, count), lambda i: (0, 0)),
        ],
        compiler_params=pltpu.CompilerParams(vmem_limit_bytes=16 << 20),
        name="scaled",
    )(notes, summed)


LIMIT = 24 << 20
SMALL = pl.CostEstimate(flops=1 << 10, bytes_accessed=1 << 10, transcendentals=0)


def terms(kernel, name, counts, rows, other, block, act=None):
    hidden = (other if act is None else act).shape[1]
    if act is None:
        hidden = hidden // 2
    first = [pltpu.VMEM((rows.shape[0], hidden), BF16)] if act is None else []
    outs = first + [pltpu.VMEM((count, block, hidden), BF16) for count in counts]
    return pl.pallas_call(
        kernel,
        out_shape=outs,
        in_specs=[whole()] * 2,
        out_specs=[whole()] * len(outs),
        compiler_params=pltpu.CompilerParams(vmem_limit_bytes=LIMIT),
        cost_estimate=SMALL,
        name=name,
    )(rows, other if act is None else act)


def open_sums(mine, theirs):
    return pl.pallas_call(
        open_kernel,
        out_shape=[pltpu.VMEM(mine.shape[1:], BF16)] * 2,
        in_specs=[whole()] * 2,
        out_specs=[whole()] * 2,
        compiler_params=pltpu.CompilerParams(vmem_limit_bytes=LIMIT),
        cost_estimate=SMALL,
        name="open_sums",
    )(mine, theirs)


def add(index, mine, theirs, moved):
    return pl.pallas_call(
        functools.partial(add_kernel, index),
        out_shape=pltpu.VMEM(moved.shape, BF16),
        in_specs=[whole()] * 3,
        out_specs=whole(),
        compiler_params=pltpu.CompilerParams(vmem_limit_bytes=LIMIT),
        cost_estimate=SMALL,
        name="add",
    )(mine, theirs, moved)


def tie(*values):
    return lax.optimization_barrier(values)


def swap(x, size):
    return lax.ppermute(x, "ed", [(i, i ^ 1) for i in range(size)])


def hop(x, size, cross=0):
    return lax.ppermute(
        x, "ed", [(i, ((i + 2 - 4 * (i % 2)) % size) ^ cross) for i in range(size)]
    )


def body(out_grad, routes, gates, pre_acts, down_weight, history):
    n_src, cap = pre_acts.shape[2], pre_acts.shape[3]
    width_ff, width = down_weight.shape[1:]
    n_ep = lax.axis_size("ep")
    n_ed = lax.axis_size("ed")
    rows_in = n_src * cap
    rows = width // n_ed

    def exchange(x):
        moved = lax.all_to_all(
            x.reshape(n_ep, cap, x.shape[1]), "ep", split_axis=0, concat_axis=0, tiled=True
        )
        return moved.reshape(rows_in, x.shape[1])

    send, inverse0, inverse1 = dispatch(
        *[
            pltpu.with_memory_space_constraint(x, pltpu.HBM)
            for x in (routes.T, gates.T, out_grad)
        ],
        n_ep,
        cap,
        n_ed,
    )
    arrived = exchange(send)
    arrived, pre_acts, down_weight, history = tie(arrived, pre_acts, down_weight, history)

    pre_block = pre_acts[0, 0].reshape(rows_in, 2 * width_ff)
    arrived, pre_block, weight = [
        pltpu.with_memory_space_constraint(x, pltpu.VMEM)
        for x in (arrived, pre_block, down_weight[0])
    ]
    act, theirs_e = terms(first_terms_kernel, "first_terms", [2], arrived, pre_block, rows)
    theirs_e = swap(theirs_e, n_ed)
    mine_e, theirs_f, mine_f = terms(
        second_terms_kernel, "second_terms", [2, 2, 2], arrived, None, rows, act
    )
    theirs_e, mine_e, theirs_f, mine_f = tie(theirs_e, mine_e, theirs_f, mine_f)
    even, odd = open_sums(mine_e, theirs_e)
    even, odd, theirs_f, arrived, act = tie(even, odd, theirs_f, arrived, act)
    even, odd = hop(even, n_ed), hop(odd, n_ed)
    theirs_f = swap(theirs_f, n_ed)
    theirs, mine = terms(
        functools.partial(last_terms_kernel, 4), "last_terms", [4, 4], arrived, None, rows, act
    )
    theirs, mine, arrived = tie(theirs, mine, arrived)
    theirs = swap(theirs, n_ed)
    pre_grad, score = gradients(arrived, pre_block, weight, n_ed)
    even, theirs_f, mine, score = tie(even, theirs_f, mine, score)

    even = hop(add(0, mine_f, theirs_f, even), n_ed)
    odd = add(1, mine_f, theirs_f, odd)
    odd, score = tie(odd, score)
    odd = hop(odd, n_ed)
    turned = [*range(n_ep // 2, n_ep), *range(n_ep // 2)]
    returned = lax.all_to_all(
        score.reshape(n_ep, cap, LANES),
        "ep",
        split_axis=0,
        concat_axis=0,
        tiled=True,
        axis_index_groups=[turned],
    ).reshape(rows_in, LANES)
    even, returned, theirs = tie(even, returned, theirs)

    even = hop(add(0, mine, theirs, even), n_ed)
    odd = hop(add(1, mine, theirs, odd), n_ed, 1)
    gate_grad = jnp.stack(
        [
            jnp.sum(inverse[: rows_in // 2] * returned[rows_in // 2 :], axis=0)
            + jnp.sum(inverse[rows_in // 2 :] * returned[: rows_in // 2], axis=0)
            for inverse in (inverse0, inverse1)
        ]
    ).T
    even, gate_grad = tie(even, gate_grad)
    even = hop(add(2, mine, theirs, even), n_ed)

    summed, note = finish(history[0], mine, theirs, even, odd, n_ed)
    high, low = range(n_ed // 4, n_ed // 2), range(n_ed // 4)
    listed = [2 * place + core for core in (1, 0) for place in (*high, *low)]
    notes = lax.all_to_all(
        note,
        "ed",
        split_axis=0,
        concat_axis=0,
        tiled=True,
        axis_index_groups=[listed],
    )
    wgrad, new_history = scaled(notes, summed, history.shape[2])
    return (pre_grad.reshape(pre_acts.shape), wgrad[None], new_history, gate_grad)


def solution(mesh):
    placed = (
        P(("ed", "ep"), None),
        P(("ed", "ep"), None),
        P(("ed", "ep"), None),
        P("ed", "ep", None, None, None),
        P("ep", None, None),
        P("ed", "ep", None),
    )
    return jax.shard_map(
        body,
        mesh=mesh,
        in_specs=placed,
        out_specs=(
            P("ed", "ep", None, None, None),
            P("ep", "ed", None),
            P("ep", None),
            P(("ed", "ep"), None),
        ),
        check_vma=False,
    )
```
